32 devices in a mesh: grp: 2 (over y), seq: 8 (over z, x), head: 2 (over core).
Axes of the slice: x: 2, y: 2, z: 4, core: 2. Of those that a mesh axis runs over, the one named last changes fastest.
Arguments:
- query_nope: bfloat16 [2048, 8192], P(('grp', 'seq'), 'head'), parts along dimension 0, may hold values from -12 to 12
- query_rope: bfloat16 [2048, 4096], P(('grp', 'seq'), 'head'), parts along dimension 0, may hold values from -400 to 400
- latents: bfloat16 [2048, 576], P(('grp', 'seq')), parts along dimension 0, may hold values from -6 to 6
- key_up: bfloat16 [512, 8192], P('seq', 'head'), may hold values from -0.25 to 0.25
- value_up: bfloat16 [512, 8192], P('seq', 'head'), may hold values from -1 to 1
- query_offset: int32 [16], P(('grp', 'seq')), parts along dimension 0, may hold values from 0 to 2047, as said below
- context_offset: int32 [16], P(('grp', 'seq')), parts along dimension 0, may hold values from 0 to 1920, as said below
Outputs:
- attention: bfloat16 [2048, 8192], P(('grp', 'seq'), 'head'), parts along dimension 0
The draws below stay inside these ranges and needn't reach their ends.
There are 2 independent parts, one for each index of `grp`. The reference program is written for one: setup_inputs(seed, part) draws one part's arguments, and reference() takes and returns one part's arrays. A program takes and returns all parts, laid end to end along the dimension named above; an argument that names none is the same for every part. Nothing has to cross between parts.
Inputs may be any that keep to these rules, and one draw needn't show every extreme that they name: context_offset[s] + 128 <= context_offset[s + 1] for every block s. context_offset[s] <= query_offset[s] < context_offset[s] + 128 for every block s.
All inputs are finite; a program needn't handle non-finite values.
Results may differ from the reference program's by a relative error of at most 0.0068.
Values may be sent and summed in bfloat16 or wider, within the bound.
A program may use at most 64 MiB of HBM per device.

```python
import math
import jax
import jax.numpy as jnp
from jax import lax

LATENT = 512
ROPE = 64
HEAD_DIM = 128
HEADS = 64
STEPS = 2
TQ_DEV = 128
KV_DEV = 128
TOKENS = 1024
CONTEXT = 1024
N_SEQ = 8


def rope_rows(key):
    return jnp.clip(jax.random.normal(key, (CONTEXT, ROPE), jnp.float32), -6.0, 6.0)


def offset_jitter(key):
    jitter = jax.random.randint(key, (N_SEQ,), 0, KV_DEV + 1)
    return jitter.at[0].set(0).at[N_SEQ - 1].set(KV_DEV)


def draw_latents(key, part):
    rope_base = rope_rows(key)
    key = jax.random.fold_in(key, 11)
    latent_cols = jnp.clip(jax.random.normal(key, (CONTEXT, LATENT), jnp.float32), -6.0, 6.0)
    return jnp.concatenate([latent_cols, rope_base], 1).astype(jnp.bfloat16)


def draw_query_rope(key, part):
    key = jax.random.fold_in(key, 23)
    noise_key = jax.random.fold_in(key, 0)
    drawn = jnp.clip(jax.random.normal(noise_key, (TOKENS, HEADS * ROPE), jnp.float32), -6.0, 6.0)
    return drawn.astype(jnp.bfloat16)


def draw_context_offset(key, part):
    jitter = offset_jitter(key)
    return (2 * KV_DEV * jnp.arange(N_SEQ, dtype=jnp.int32) + jitter).astype(jnp.int32)


def draw_query_offset(key, part):
    jitter = offset_jitter(key)
    key = jax.random.fold_in(key, 37)
    inside = jax.random.randint(key, (N_SEQ,), 0, KV_DEV)
    inside = inside.at[0].set(0).at[N_SEQ - 1].set(KV_DEV - 1)
    return (2 * KV_DEV * jnp.arange(N_SEQ, dtype=jnp.int32) + jitter + inside).astype(jnp.int32)


def block_levels(rng, dims, shards, low, high):
    level = 1.0
    for position, parts in shards:
        heights = jax.random.uniform(jax.random.fold_in(jax.random.fold_in(rng, 6), position), (parts,), jnp.float32, low / len(shards), high / len(shards))
        level = level * jnp.repeat(jnp.exp(heights), dims[position] // parts).reshape((-1,) + (1,) * (len(dims) - 1 - position))
    return level


def normal_values(key, dims, scale, bound, cuts=(), held_as=jnp.bfloat16):
    loudness = block_levels(key, dims, cuts, -0.22, 0.18) if cuts else 1.0
    entries = jax.random.normal(key, dims, jnp.float32) * scale * loudness
    return jnp.minimum(jnp.maximum(entries, -bound), bound).astype(held_as)


def setup_inputs(seed: int = 0, part: int = 0) -> dict:
    key_of = jax.random.split(jax.random.key(seed), 8)
    part_keys = jax.random.split(jax.random.fold_in(key_of[7], part), 8)
    query_nope = normal_values(part_keys[0], (TOKENS, HEADS * HEAD_DIM), 2.0, 12.0, ((0, 8), (1, 2)))
    query_rope = draw_query_rope(jax.random.fold_in(jax.random.fold_in(key_of[7], part), 71), part)
    latents = draw_latents(jax.random.fold_in(jax.random.fold_in(key_of[7], part), 71), part)
    key_up = normal_values(key_of[3], (LATENT, HEADS * HEAD_DIM), LATENT ** -0.5, 0.25, ((0, 8), (1, 2)))
    value_up = normal_values(key_of[4], (LATENT, HEADS * HEAD_DIM), (LATENT // 16) ** -0.5, 1.0, ((0, 8), (1, 2)))
    query_offset = draw_query_offset(jax.random.fold_in(jax.random.fold_in(key_of[7], part), 71), part)
    context_offset = draw_context_offset(jax.random.fold_in(jax.random.fold_in(key_of[7], part), 71), part)
    return dict(query_nope=query_nope, query_rope=query_rope, latents=latents, key_up=key_up, value_up=value_up, query_offset=query_offset, context_offset=context_offset)


def reference(query_nope, query_rope, latents, key_up, value_up, query_offset, context_offset):
    latent_cols = latents[:, :LATENT]
    key_rows = jnp.dot(latent_cols, key_up, preferred_element_type=jnp.float32).astype(jnp.bfloat16)
    value_rows = jnp.dot(latent_cols, value_up, preferred_element_type=jnp.float32).astype(jnp.bfloat16)
    rope_keys = latents[:, LATENT:]
    softmax_scale = 1.0 / math.sqrt(HEAD_DIM + ROPE)

    def one_block(block_index):
        row_start = block_index * TQ_DEV
        query_part = lax.dynamic_slice_in_dim(query_nope, row_start, TQ_DEV, 0).astype(jnp.float32)
        query_part = query_part.reshape(TQ_DEV, HEADS, HEAD_DIM)
        rotary_part = lax.dynamic_slice_in_dim(query_rope, row_start, TQ_DEV, 0).astype(jnp.float32)
        rotary_part = rotary_part.reshape(TQ_DEV, HEADS, ROPE)
        first_query = lax.dynamic_slice_in_dim(query_offset, block_index, 1, 0)[0]
        query_place = first_query + jnp.arange(TQ_DEV, dtype=jnp.int32)
        key_list = []
        value_list = []
        rope_list = []
        place_list = []
        for distance in range(STEPS + 1):
            source = ((block_index - distance) % N_SEQ).astype(jnp.int32)
            source_start = (source * KV_DEV).astype(jnp.int32)
            key_list.append(lax.dynamic_slice_in_dim(key_rows, source_start, KV_DEV, 0))
            value_list.append(lax.dynamic_slice_in_dim(value_rows, source_start, KV_DEV, 0))
            rope_list.append(lax.dynamic_slice_in_dim(rope_keys, source_start, KV_DEV, 0))
            first_key = lax.dynamic_slice_in_dim(context_offset, source, 1, 0)[0]
            turn_back = jnp.where(source > block_index, jnp.int32(2 * KV_DEV * N_SEQ), jnp.int32(0))
            place_list.append(first_key - turn_back + jnp.arange(KV_DEV, dtype=jnp.int32))
        block_keys = jnp.concatenate(key_list, 0).astype(jnp.float32).reshape(-1, HEADS, HEAD_DIM)
        block_values = jnp.concatenate(value_list, 0).astype(jnp.float32).reshape(-1, HEADS, HEAD_DIM)
        block_rope = jnp.concatenate(rope_list, 0).astype(jnp.float32)
        key_place = jnp.concatenate(place_list, 0)
        scores = jnp.einsum('qhd,khd->hqk', query_part, block_keys)
        scores = (scores + jnp.einsum('qhr,kr->hqk', rotary_part, block_rope)) * softmax_scale
        visible = key_place[None, None, :] <= query_place[None, :, None]
        scores = jnp.where(visible, scores, jnp.float32(-1e+30))
        highest = lax.optimization_barrier(jnp.max(scores, axis=2, keepdims=True))
        numerator = jnp.where(visible, jnp.exp(scores - highest), jnp.float32(0.0))
        denominator = lax.optimization_barrier(jnp.sum(numerator, axis=2, keepdims=True))
        weights_bf = (numerator / denominator).astype(jnp.bfloat16)
        output = jnp.einsum('hqk,khd->qhd', weights_bf.astype(jnp.float32), block_values)
        return output.reshape(TQ_DEV, HEADS * HEAD_DIM).astype(jnp.bfloat16)
    outputs = lax.map(one_block, jnp.arange(N_SEQ, dtype=jnp.int32))
    return outputs.reshape(TOKENS, HEADS * HEAD_DIM)
```

```python
import functools
import math

import jax
import jax.numpy as jnp
from jax import lax
from jax.experimental import pallas as pl
from jax.experimental.pallas import tpu as pltpu
from jax.sharding import PartitionSpec as P

LATENT = 512
ROPE = 64
HEAD_DIM = 128
STEPS = 2
CHUNK_HEADS = 4
MESH = pl.DeviceIdType.MESH


def shifted(x, axis, by):
    peers = lax.axis_size(axis)
    return lax.ppermute(x, axis, [(i, (i + by) % peers) for i in range(peers)])


def fetch_block(latent_block, distance):
    return shifted(latent_block, "seq", distance)


def local_general(query_nope, query_rope, latents, key_up, value_up, query_offset, context_offset):
    query_rows = query_nope.shape[0]
    kv_rows = latents.shape[0]
    local_heads = key_up.shape[1] // HEAD_DIM
    blocks = [latents]
    for distance in range(STEPS):
        blocks.append(fetch_block(blocks[-1], 1))
    context = jnp.concatenate(blocks, 0)
    latent_cols = context[:, :LATENT]
    rope_keys = context[:, LATENT:]
    key_full, value_full = (
        lax.all_gather(key_up, "seq", axis=0, tiled=True),
        lax.all_gather(value_up, "seq", axis=0, tiled=True),
    )
    key_sums = jnp.dot(latent_cols, key_full, preferred_element_type=jnp.float32)
    value_sums = jnp.dot(latent_cols, value_full, preferred_element_type=jnp.float32)
    key_rows = key_sums.astype(jnp.bfloat16).reshape(-1, local_heads, HEAD_DIM)
    value_rows = value_sums.astype(jnp.bfloat16).reshape(-1, local_heads, HEAD_DIM)
    query_part = query_nope.reshape(query_rows, local_heads, HEAD_DIM)
    rotary_part = query_rope.reshape(query_rows, local_heads, ROPE)
    softmax_scale = 1.0 / math.sqrt(HEAD_DIM + ROPE)
    scores = jnp.einsum("qhd,khd->hqk", query_part, key_rows, preferred_element_type=jnp.float32)
    scores = (
        scores
        + jnp.einsum("qhr,kr->hqk", rotary_part, rope_keys, preferred_element_type=jnp.float32)
    ) * softmax_scale
    query_place = query_offset[0] + jnp.arange(query_rows, dtype=jnp.int32)
    own_place = context_offset[0] + jnp.arange(kv_rows, dtype=jnp.int32)
    mask_list = [own_place[None, :] <= query_place[:, None]]
    for distance in range(STEPS):
        mask_list.append(jnp.ones((query_rows, kv_rows), dtype=bool))
    visible = jnp.concatenate(mask_list, 1)[None, :, :]
    scores = jnp.where(visible, scores, jnp.float32(-1e30))
    highest = jnp.max(scores, axis=2, keepdims=True)
    numerator = jnp.where(visible, jnp.exp(scores - highest), jnp.float32(0.0))
    denominator = jnp.sum(numerator, axis=2, keepdims=True)
    weights_bf = (numerator / denominator).astype(jnp.bfloat16)
    output = jnp.einsum("hqk,khd->qhd", weights_bf, value_rows, preferred_element_type=jnp.float32)
    return output.reshape(query_rows, local_heads * HEAD_DIM).astype(jnp.bfloat16)


def kernel(
    pairs, chunks, qn, qr, lat, ku, vu, off, out,
    w, q, r, blocks, offs, context, ropes, o,
    own_w, own_q, own_r, own_small, own_o,
    xw_s, xw_r, xq_s, xq_r, xr_s, xr_r, small_s, small_r,
    right_s, right_r, left_s, left_r, yw_s, yw_r, xo_s, xo_r,
):
    g, s, c = lax.axis_index("grp"), lax.axis_index("seq"), lax.axis_index("head")
    z, x = s // 2, s % 2
    mate = 2 * z + 1 - x
    shard = ku.shape[0]
    width = w.shape[3]
    rope_width = r.shape[3]
    half = chunks * width
    rope_half = chunks * rope_width
    to_mate = (g, mate, c)
    to_group = (1 - g, s, c)
    to_right = (g, 2 * ((z + 1) % pairs) + x, c)
    to_left = (g, 2 * ((z + pairs - 1) % pairs) + x, c)

    def remote(src, dst, send, recv, device):
        return pltpu.make_async_remote_copy(
            src_ref=src, dst_ref=dst, send_sem=send, recv_sem=recv, device_id=device, device_id_type=MESH
        )

    def cols(h, j):
        return pl.ds(pl.multiple_of(h * half + j * width, 128), width)

    def rope_cols(h, j):
        return pl.ds(pl.multiple_of(h * rope_half + j * rope_width, 128), rope_width)

    def rows(first, count):
        return pl.ds(pl.multiple_of(first, 16), count)

    def own_copies(j):
        mine = rows(s * shard, shard)
        return (
            pltpu.make_async_copy(ku.at[:, cols(x, j)], w.at[0, j, mine, :], own_w.at[0, j]),
            pltpu.make_async_copy(vu.at[:, cols(x, j)], w.at[1, j, mine, :], own_w.at[1, j]),
        )

    def own_query(j):
        return (
            pltpu.make_async_copy(qn.at[:, cols(x, j)], q.at[x, j], own_q.at[j]),
            pltpu.make_async_copy(qr.at[:, rope_cols(x, j)], r.at[x, j], own_r.at[j]),
        )

    def mate_weights(j, src):
        return remote(
            src.at[:, cols(1 - x, j)], w.at[g, j, rows(s * shard, shard), :], xw_s.at[j], xw_r.at[j], to_mate
        )

    def mate_query(j):
        return (
            remote(qn.at[:, cols(1 - x, j)], q.at[x, j], xq_s.at[j], xq_r.at[j], to_mate),
            remote(qr.at[:, rope_cols(1 - x, j)], r.at[x, j], xr_s.at[j], xr_r.at[j], to_mate),
        )

    def payload(j, place):
        return w.at[g, j, rows(place * 2 * shard, 2 * shard), :]

    def go_right(j, d):
        ref = payload(j, z - d + 1)
        return remote(ref, ref, right_s.at[j, d], right_r.at[j, d], to_right)

    def go_left(j, d):
        ref = payload(j, z + d - 1)
        return remote(ref, ref, left_s.at[j, d], left_r.at[j, d], to_left)

    def across_mate(j):
        ref = w.at[g, j, rows(mate * shard, shard), :]
        return remote(ref, ref, yw_s.at[j, 0], yw_r.at[j, 0], to_group)

    def across(j, place, slot):
        ref = payload(j, place)
        return remote(ref, ref, yw_s.at[j, slot], yw_r.at[j, slot], to_group)

    own_small_copies = (
        pltpu.make_async_copy(lat, blocks.at[2 + x], own_small.at[0]),
        pltpu.make_async_copy(off, offs.at[x], own_small.at[1]),
    )
    lat_mate = remote(lat, blocks.at[2 + x], small_s.at[0], small_r.at[0], to_mate)
    off_mate = remote(off, offs.at[x], small_s.at[1], small_r.at[1], to_mate)
    lat_right = remote(lat, blocks.at[x], small_s.at[2], small_r.at[2], to_right)
    lat_on = remote(blocks.at[x], blocks.at[x], small_s.at[3], small_r.at[3], to_mate)

    def result_own(j):
        return pltpu.make_async_copy(o.at[x, j], out.at[:, cols(x, j)], own_o.at[j])

    def result_mate(j):
        return remote(o.at[1 - x, j], out.at[:, cols(x, j)], xo_s.at[j], xo_r.at[j], to_mate)

    def start_own(j, carry):
        for copy in own_copies(j):
            copy.start()
        return carry

    lax.fori_loop(0, chunks, start_own, 0)
    for copy in own_small_copies:
        copy.start()

    barrier = pltpu.get_barrier_semaphore()
    for device in (to_mate, to_group, to_right, to_left):
        pl.semaphore_signal(barrier, inc=1, device_id=device, device_id_type=MESH)
    pl.semaphore_wait(barrier, 4)

    def start_mate(j, carry):
        @pl.when(g == 0)
        def _():
            mate_weights(j, ku).start()

        @pl.when(g != 0)
        def _():
            mate_weights(j, vu).start()

        return carry

    lax.fori_loop(0, chunks, start_mate, 0)
    lat_right.start()
    lat_mate.start()
    off_mate.start()

    def enter(j):
        for copy in own_query(j) + mate_query(j):
            copy.start()
        for copy in own_copies(j):
            copy.wait()
        mate_weights(j, ku).wait_recv()

        @pl.when(z + 1 < pairs)
        def _():
            go_right(j, 1).start()

        @pl.when(z > 0)
        def _():
            go_left(j, 1).start()

        across_mate(j).start()

    def hand_on(j, d):
        @pl.when(z >= d)
        def _():
            go_right(j, d).wait_recv()

            @pl.when(z + 1 < pairs)
            def _():
                if d + 1 < pairs:
                    go_right(j, d + 1).start()

            across(j, z - d, d).start()

        @pl.when(z + d < pairs)
        def _():
            go_left(j, d).wait_recv()

            @pl.when(z > 0)
            def _():
                if d + 1 < pairs:
                    go_left(j, d + 1).start()

            across(j, z + d, pairs - 1 + d).start()

    def for_arrivals(j, method):
        getattr(across_mate(j), method)()
        for d in range(1, pairs):
            @pl.when(z >= d)
            def _():
                getattr(across(j, z - d, d), method)()

            @pl.when(z + d < pairs)
            def _():
                getattr(across(j, z + d, pairs - 1 + d), method)()

    def prepare():
        lat_on.wait_recv()
        lat_mate.wait_recv()
        off_mate.wait_recv()
        for copy in own_small_copies:
            copy.wait()
        kv = lat.shape[0]
        none = jnp.zeros((kv, ROPE), jnp.bfloat16)
        for k in range(4):
            context[k * kv:(k + 1) * kv, :] = blocks[k, :, :LATENT]
            rope_keys = blocks[k, :, LATENT:]
            ropes[0, k * kv:(k + 1) * kv, :] = jnp.concatenate([rope_keys, none], 1)
            ropes[1, k * kv:(k + 1) * kv, :] = jnp.concatenate([none, rope_keys], 1)

    def attend(j):
        for copy in own_query(j):
            copy.wait()
        for copy in mate_query(j):
            copy.wait_recv()
        kv = lat.shape[0]
        tokens = qn.shape[0]
        keys = jnp.dot(context[...], w[0, j], preferred_element_type=jnp.float32).astype(jnp.bfloat16)
        values = jnp.dot(context[...], w[1, j], preferred_element_type=jnp.float32).astype(jnp.bfloat16)
        factor = math.log2(math.e) / math.sqrt(HEAD_DIM + ROPE)
        token = lax.broadcasted_iota(jnp.int32, (tokens, kv), 0)
        row = lax.broadcasted_iota(jnp.int32, (tokens, kv), 1)
        for b in range(2):
            seen = slice(b * kv, (b + 1 + STEPS) * kv)
            visible = row <= token + offs[b, 0:1, :]
            for h in range(width // HEAD_DIM):
                lanes = slice(h * HEAD_DIM, (h + 1) * HEAD_DIM)
                pair_lanes = slice(h // 2 * 2 * ROPE, (h // 2 + 1) * 2 * ROPE)
                query = jnp.concatenate([q[b, j, :, lanes], r[b, j, :, pair_lanes]], 1)
                key = jnp.concatenate([keys[seen, lanes], ropes[h % 2, seen, :]], 1)
                scores = lax.dot_general(query, key, (((1,), (1,)), ((), ())), preferred_element_type=jnp.float32)
                scores = jnp.concatenate(
                    [scores[:, :STEPS * kv], jnp.where(visible, scores[:, STEPS * kv:], jnp.float32(-1e30))], 1
                )
                highest = jnp.max(scores, axis=1, keepdims=True)
                numerator = jnp.exp2((scores - highest) * factor)
                inverse = 1.0 / jnp.sum(numerator, axis=1, keepdims=True)
                weights = (numerator * inverse).astype(jnp.bfloat16)
                summed = jnp.dot(weights, values[seen, lanes], preferred_element_type=jnp.float32)
                o[b, j, :, lanes] = summed.astype(jnp.bfloat16)
        result_mate(j).start()
        result_own(j).start()

    def step(t, carry):
        @pl.when(t < chunks)
        def _():
            enter(t)

        @pl.when(t == 0)
        def _():
            lat_right.wait_recv()
            lat_on.start()

        for d in range(1, pairs):
            @pl.when((t >= d) & (t < chunks + d))
            def _():
                hand_on(t - d, d)

        @pl.when(t == pairs)
        def _():
            prepare()

        @pl.when(t >= pairs)
        def _():
            for_arrivals(t - pairs, "wait_recv")
            attend(t - pairs)

        return carry

    lax.fori_loop(0, chunks + pairs, step, 0)

    lat_right.wait_send()
    lat_mate.wait_send()
    off_mate.wait_send()
    lat_on.wait_send()

    def finish(j, carry):
        mate_weights(j, ku).wait_send()
        for copy in mate_query(j):
            copy.wait_send()
        for d in range(1, pairs):
            @pl.when((z >= d - 1) & (z + 1 < pairs))
            def _():
                go_right(j, d).wait_send()

            @pl.when((z + d - 1 < pairs) & (z > 0))
            def _():
                go_left(j, d).wait_send()

        for_arrivals(j, "wait_send")
        result_own(j).wait()
        result_mate(j).wait()
        return carry

    lax.fori_loop(0, chunks, finish, 0)


def local_pairs(n_seq, query_nope, query_rope, latents, key_up, value_up, query_offset, context_offset):
    tokens = query_nope.shape[0]
    kv = latents.shape[0]
    heads = key_up.shape[1] // HEAD_DIM
    pairs = n_seq // 2
    chunks = heads // 2 // CHUNK_HEADS
    width = CHUNK_HEADS * HEAD_DIM
    rope_width = CHUNK_HEADS * ROPE
    ahead = jnp.broadcast_to((query_offset - context_offset)[:, None], (8, kv))
    dma = pltpu.SemaphoreType.DMA
    bf16 = jnp.bfloat16
    slots = 2 * pairs - 1
    return pl.pallas_call(
        functools.partial(kernel, pairs, chunks),
        out_shape=jax.ShapeDtypeStruct(query_nope.shape, bf16),
        in_specs=[pl.BlockSpec(memory_space=pl.ANY)] * 6,
        out_specs=pl.BlockSpec(memory_space=pl.ANY),
        scratch_shapes=[
            pltpu.VMEM((2, chunks, LATENT, width), bf16),
            pltpu.VMEM((2, chunks, tokens, width), bf16),
            pltpu.VMEM((2, chunks, tokens, rope_width), bf16),
            pltpu.VMEM((4,) + latents.shape, bf16),
            pltpu.VMEM((2, 8, kv), jnp.int32),
            pltpu.VMEM((4 * kv, LATENT), bf16),
            pltpu.VMEM((2, 4 * kv, 2 * ROPE), bf16),
            pltpu.VMEM((2, chunks, tokens, width), bf16),
            dma((2, chunks)), dma((chunks,)), dma((chunks,)), dma((2,)), dma((chunks,)),
            dma((chunks,)), dma((chunks,)), dma((chunks,)), dma((chunks,)), dma((chunks,)), dma((chunks,)),
            dma((4,)), dma((4,)),
            dma((chunks, pairs)), dma((chunks, pairs)), dma((chunks, pairs)), dma((chunks, pairs)),
            dma((chunks, slots)), dma((chunks, slots)), dma((chunks,)), dma((chunks,)),
        ],
        compiler_params=pltpu.CompilerParams(
            collective_id=0, has_side_effects=True, vmem_limit_bytes=40 * 1024 * 1024
        ),
        cost_estimate=pl.CostEstimate(flops=5 * 10 ** 9, bytes_accessed=8 * 10 ** 6, transcendentals=2 * 10 ** 6),
    )(query_nope, query_rope, latents, key_up, value_up, ahead)


def solution(mesh):
    in_specs = (
        P(("grp", "seq"), "head"),
        P(("grp", "seq"), "head"),
        P(("grp", "seq"), None),
        P("seq", "head"),
        P("seq", "head"),
        P(("grp", "seq")),
        P(("grp", "seq")),
    )
    out_specs = P(("grp", "seq"), "head")
    n_seq = mesh.shape["seq"]
    if mesh.shape["grp"] == 2 and n_seq % 2 == 0 and n_seq >= 6 and LATENT // n_seq % 16 == 0:
        local = functools.partial(local_pairs, n_seq)
    else:
        local = local_general
    return jax.shard_map(local, mesh=mesh, in_specs=in_specs, out_specs=out_specs, check_vma=False)
```

```python
import functools
import math

import jax
import jax.numpy as jnp
from jax import lax
from jax.experimental import pallas as pl
from jax.experimental.pallas import tpu as pltpu
from jax.sharding import PartitionSpec as P

LATENT = 512
ROPE = 64
HEAD_DIM = 128
STEPS = 2
CHUNK_HEADS = 2
AHEAD = 2
MESH = pl.DeviceIdType.MESH


def shifted(x, axis, by):
    peers = lax.axis_size(axis)
    return lax.ppermute(x, axis, [(i, (i + by) % peers) for i in range(peers)])


def fetch_block(latent_block, distance):
    return shifted(latent_block, "seq", distance)


def local_general(query_nope, query_rope, latents, key_up, value_up, query_offset, context_offset):
    query_rows = query_nope.shape[0]
    kv_rows = latents.shape[0]
    local_heads = key_up.shape[1] // HEAD_DIM
    blocks = [latents]
    for distance in range(STEPS):
        blocks.append(fetch_block(blocks[-1], 1))
    context = jnp.concatenate(blocks, 0)
    latent_cols = context[:, :LATENT]
    rope_keys = context[:, LATENT:]
    key_full, value_full = (
        lax.all_gather(key_up, "seq", axis=0, tiled=True),
        lax.all_gather(value_up, "seq", axis=0, tiled=True),
    )
    key_sums = jnp.dot(latent_cols, key_full, preferred_element_type=jnp.float32)
    value_sums = jnp.dot(latent_cols, value_full, preferred_element_type=jnp.float32)
    key_rows = key_sums.astype(jnp.bfloat16).reshape(-1, local_heads, HEAD_DIM)
    value_rows = value_sums.astype(jnp.bfloat16).reshape(-1, local_heads, HEAD_DIM)
    query_part = query_nope.reshape(query_rows, local_heads, HEAD_DIM)
    rotary_part = query_rope.reshape(query_rows, local_heads, ROPE)
    softmax_scale = 1.0 / math.sqrt(HEAD_DIM + ROPE)
    scores = jnp.einsum("qhd,khd->hqk", query_part, key_rows, preferred_element_type=jnp.float32)
    scores = (
        scores
        + jnp.einsum("qhr,kr->hqk", rotary_part, rope_keys, preferred_element_type=jnp.float32)
    ) * softmax_scale
    query_place = query_offset[0] + jnp.arange(query_rows, dtype=jnp.int32)
    own_place = context_offset[0] + jnp.arange(kv_rows, dtype=jnp.int32)
    mask_list = [own_place[None, :] <= query_place[:, None]]
    for distance in range(STEPS):
        mask_list.append(jnp.ones((query_rows, kv_rows), dtype=bool))
    visible = jnp.concatenate(mask_list, 1)[None, :, :]
    scores = jnp.where(visible, scores, jnp.float32(-1e30))
    highest = jnp.max(scores, axis=2, keepdims=True)
    numerator = jnp.where(visible, jnp.exp(scores - highest), jnp.float32(0.0))
    denominator = jnp.sum(numerator, axis=2, keepdims=True)
    weights_bf = (numerator / denominator).astype(jnp.bfloat16)
    output = jnp.einsum("hqk,khd->qhd", weights_bf, value_rows, preferred_element_type=jnp.float32)
    return output.reshape(query_rows, local_heads * HEAD_DIM).astype(jnp.bfloat16)


def kernel(
    pairs, chunks, q_off, c_off, qn, qr, lat, ku, vu, out,
    w, q, r, blocks, offs, context, ropes, wide, o,
    own_w, own_q, own_r, own_lat_sem, own_o,
    xw_s, xw_r, q_s, q_r, r_s, r_r, lat_s, lat_r, twin_s, twin_r, off_s, off_r,
    right_s, right_r, left_s, left_r, o_s, o_r,
):
    g, s, c = lax.axis_index("grp"), lax.axis_index("seq"), lax.axis_index("head")
    z, x = s // 2, s % 2
    me = 2 * g + x
    mate = 2 * z + 1 - x
    shard = ku.shape[0]
    width = q.shape[3]
    rope_width = r.shape[3]
    lat_half = lat.shape[0] // 2
    to_mate = (g, mate, c)
    to_right = (g, 2 * ((z + 1) % pairs) + x, c)
    to_left = (g, 2 * ((z + pairs - 1) % pairs) + x, c)
    to_twin = (g, s, 1 - c)

    def member(k):
        kg, kx = k // 2, k % 2
        return g + kg - 2 * g * kg, x + kx - 2 * x * kx

    def to_member(k):
        mg, mx = member(k)
        return (mg, 2 * z + mx, c)

    def number(k):
        mg, mx = member(k)
        return 2 * mg + mx

    def remote(src, dst, send, recv, device):
        return pltpu.make_async_remote_copy(
            src_ref=src, dst_ref=dst, send_sem=send, recv_sem=recv, device_id=device, device_id_type=MESH
        )

    def cols(quarter, j):
        return pl.ds(pl.multiple_of((quarter * chunks + j) * width, 128), width)

    def rope_cols(quarter, j):
        return pl.ds(pl.multiple_of((quarter * chunks + j) * rope_width, 128), rope_width)

    def rows(first, count):
        return pl.ds(pl.multiple_of(first, 16), count)

    def own_copies(j):
        mine = rows(s * shard, shard)
        return [
            pltpu.make_async_copy(up.at[:, cols(me, j)], w.at[j, mine, m * width:(m + 1) * width], own_w.at[m, j])
            for m, up in enumerate((ku, vu))
        ]

    def mate_weights(j):
        mine = rows(s * shard, shard)
        quarter = 2 * g + 1 - x
        return [
            remote(
                up.at[:, cols(quarter, j)], w.at[j, mine, m * width:(m + 1) * width], xw_s.at[m, j], xw_r.at[m, j],
                to_mate,
            )
            for m, up in enumerate((ku, vu))
        ]

    def own_query(j):
        return [
            pltpu.make_async_copy(qn.at[:, cols(me, j)], q.at[me, j], own_q.at[j]),
            pltpu.make_async_copy(qr.at[:, rope_cols(me, j)], r.at[me, j], own_r.at[j]),
        ]

    def member_query(j):
        copies = []
        for k in range(1, 4):
            copies.append(remote(qn.at[:, cols(number(k), j)], q.at[me, j], q_s.at[k, j], q_r.at[k, j], to_member(k)))
            copies.append(remote(qr.at[:, rope_cols(number(k), j)], r.at[me, j], r_s.at[k, j], r_r.at[k, j], to_member(k)))
        return copies

    def payload(j, place):
        return w.at[j, rows(place * 2 * shard, 2 * shard), :]

    def go_right(j, d, source=None):
        if source is not None:
            ref = w.at[j, rows(source * shard, shard), :]
            slot = pairs * (source % 2)
            return remote(ref, ref, right_s.at[j, slot], right_r.at[j, slot], to_right)
        ref = payload(j, z - d + 1)
        return remote(ref, ref, right_s.at[j, d], right_r.at[j, d], to_right)

    def go_left(j, d, source=None):
        if source is not None:
            ref = w.at[j, rows(source * shard, shard), :]
            slot = pairs * (source % 2)
            return remote(ref, ref, left_s.at[j, slot], left_r.at[j, slot], to_left)
        ref = payload(j, z + d - 1)
        return remote(ref, ref, left_s.at[j, d], left_r.at[j, d], to_left)

    def place(k, current):
        mg, mx = member(k)
        return 4 * mg + 2 * current + mx

    def own_part(ref):
        return ref.at[rows(c * lat_half, lat_half), :]

    own_lat = pltpu.make_async_copy(lat, blocks.at[place(0, 1)], own_lat_sem)
    lat_right = remote(own_part(lat), own_part(blocks.at[place(0, 0)]), lat_s.at[0, 0], lat_r.at[0, 0], to_right)

    def lat_member(k, current):
        src = own_part(lat) if current else own_part(blocks.at[place(0, 0)])
        return remote(src, own_part(blocks.at[place(0, current)]), lat_s.at[k, current], lat_r.at[k, current], to_member(k))

    def lat_twin(k, current):
        ref = own_part(blocks.at[place(k, current)])
        return remote(ref, ref, twin_s.at[k, current], twin_r.at[k, current], to_twin)

    def off_member(k):
        return remote(offs.at[me], offs.at[me], off_s.at[k], off_r.at[k], to_member(k))

    def result_own(j):
        return pltpu.make_async_copy(o.at[me, j], out.at[:, cols(me, j)], own_o.at[j])

    def result_member(j, k):
        return remote(o.at[number(k), j], out.at[:, cols(me, j)], o_s.at[k, j], o_r.at[k, j], to_member(k))

    def start_own(j, carry):
        for copy in own_copies(j):
            copy.start()
        return carry

    lax.fori_loop(0, chunks, start_own, 0)
    own_lat.start()
    offs[me] = jnp.full(offs.shape[1:], q_off[0] - c_off[0], jnp.int32)

    barrier = pltpu.get_barrier_semaphore()
    for device in [to_member(k) for k in range(1, 4)] + [to_right, to_left, to_twin]:
        pl.semaphore_signal(barrier, inc=1, device_id=device, device_id_type=MESH)
    pl.semaphore_wait(barrier, 6)

    def start_mate(j, carry):
        for copy in mate_weights(j):
            copy.start()
        return carry

    def send(j, source):
        @pl.when(z + 1 < pairs)
        def _():
            go_right(j, 1, source).start()

        @pl.when(z > 0)
        def _():
            go_left(j, 1, source).start()

    def enter(j):
        for copy in own_copies(j):
            copy.wait()
        send(j, s)
        for copy in own_query(j) + member_query(j):
            copy.start()

    def pass_mate(j):
        for copy in mate_weights(j):
            copy.wait_recv()
        send(j, mate)

    def first(j, carry):
        enter(j)
        return carry

    def second(j, carry):
        pass_mate(j)
        return carry

    lax.fori_loop(0, chunks, start_mate, 0)
    lat_right.start()
    for k in range(1, 4):
        lat_member(k, 1).start()
        off_member(k).start()
    lax.fori_loop(0, AHEAD, first, 0)
    lax.fori_loop(0, AHEAD, second, 0)

    def hand_on(j, d):
        @pl.when(z >= d)
        def _():
            if d == 1:
                go_right(j, d, s).wait_recv()
                go_right(j, d, mate).wait_recv()
            else:
                go_right(j, d).wait_recv()

            @pl.when(z + 1 < pairs)
            def _():
                if d + 1 < pairs:
                    go_right(j, d + 1).start()

        @pl.when(z + d < pairs)
        def _():
            if d == 1:
                go_left(j, d, s).wait_recv()
                go_left(j, d, mate).wait_recv()
            else:
                go_left(j, d).wait_recv()

            @pl.when(z > 0)
            def _():
                if d + 1 < pairs:
                    go_left(j, d + 1).start()

    def spread_previous():
        lat_right.wait_recv()
        for k in range(1, 4):
            lat_member(k, 0).start()
        lat_twin(0, 0).start()

    def spread_twin():
        for k in range(1, 4):
            for current in (1, 0):
                lat_member(k, current).wait_recv()
                lat_twin(k, current).start()

    def prepare():
        own_lat.wait()
        lat_twin(0, 0).wait_recv()
        for k in range(1, 4):
            off_member(k).wait_recv()
            for current in (1, 0):
                lat_twin(k, current).wait_recv()
        kv = lat.shape[1]
        none = jnp.zeros((kv, ROPE), jnp.bfloat16)
        for k in range(8):
            context[k * kv:(k + 1) * kv, :] = blocks[k, :LATENT, :].T
            rope_keys = blocks[k, LATENT:, :].T
            ropes[0, k * kv:(k + 1) * kv, :] = jnp.concatenate([rope_keys, none], 1)
            ropes[1, k * kv:(k + 1) * kv, :] = jnp.concatenate([none, rope_keys], 1)
        wide[:, :, HEAD_DIM:] = jnp.ones((wide.shape[0], 8 * kv, HEAD_DIM), jnp.bfloat16)

    def attend(j):
        for copy in own_query(j):
            copy.wait()
        for copy in member_query(j):
            copy.wait_recv()
        kv = lat.shape[1]
        tokens = qn.shape[0]
        both = jnp.dot(context[...], w[j], preferred_element_type=jnp.float32).astype(jnp.bfloat16)
        for h in range(width // HEAD_DIM):
            wide[h, :, :HEAD_DIM] = both[:, width + h * HEAD_DIM:width + (h + 1) * HEAD_DIM]
        factor = math.log2(math.e) / math.sqrt(HEAD_DIM + ROPE)
        token = lax.broadcasted_iota(jnp.int32, (tokens, kv), 0)
        row = lax.broadcasted_iota(jnp.int32, (tokens, kv), 1)
        for b in range(4):
            start = (4 * (b // 2) + b % 2) * kv
            seen = slice(start, start + (1 + STEPS) * kv)
            visible = row <= token + offs[b, 0:1, :]
            for h in range(width // HEAD_DIM):
                lanes = slice(h * HEAD_DIM, (h + 1) * HEAD_DIM)
                pair_lanes = slice(h // 2 * 2 * ROPE, (h // 2 + 1) * 2 * ROPE)
                query = jnp.concatenate([q[b, j, :, lanes], r[b, j, :, pair_lanes]], 1)
                key = jnp.concatenate([both[seen, lanes], ropes[h % 2, seen, :]], 1)
                scores = lax.dot_general(query, key, (((1,), (1,)), ((), ())), preferred_element_type=jnp.float32)
                scores = jnp.concatenate(
                    [scores[:, :STEPS * kv], jnp.where(visible, scores[:, STEPS * kv:], jnp.float32(-1e30))], 1
                )
                highest = jnp.max(scores, axis=1, keepdims=True)
                numerator = jnp.exp2((scores - highest) * factor).astype(jnp.bfloat16)
                summed = jnp.dot(numerator, wide[h, seen, :], preferred_element_type=jnp.float32)
                o[b, j, :, lanes] = (summed[:, :HEAD_DIM] / summed[:, HEAD_DIM:]).astype(jnp.bfloat16)
        for k in range(3, 0, -1):
            result_member(j, k).start()
        result_own(j).start()

    def step(t, carry):
        @pl.when(t + AHEAD < chunks)
        def _():
            enter(t + AHEAD)
            pass_mate(t + AHEAD)

        @pl.when(t == 0)
        def _():
            spread_previous()

        for d in range(1, pairs):
            @pl.when((t >= d) & (t < chunks + d))
            def _():
                hand_on(t - d, d)

        @pl.when(t == 1)
        def _():
            spread_twin()

        @pl.when(t == pairs - 1)
        def _():
            prepare()

        @pl.when(t >= pairs - 1)
        def _():
            attend(t - pairs + 1)

        return carry

    lax.fori_loop(0, chunks + pairs - 1, step, 0)

    lat_right.wait_send()
    lat_twin(0, 0).wait_send()
    for k in range(1, 4):
        off_member(k).wait_send()
        for current in (1, 0):
            lat_member(k, current).wait_send()
            lat_twin(k, current).wait_send()

    def finish(j, carry):
        for copy in mate_weights(j) + member_query(j):
            copy.wait_send()
        for d in range(1, pairs):
            @pl.when((z >= d - 1) & (z + 1 < pairs))
            def _():
                if d == 1:
                    go_right(j, d, s).wait_send()
                    go_right(j, d, mate).wait_send()
                else:
                    go_right(j, d).wait_send()

            @pl.when((z + d - 1 < pairs) & (z > 0))
            def _():
                if d == 1:
                    go_left(j, d, s).wait_send()
                    go_left(j, d, mate).wait_send()
                else:
                    go_left(j, d).wait_send()

        result_own(j).wait()
        for k in range(1, 4):
            result_member(j, k).wait()
        return carry

    lax.fori_loop(0, chunks, finish, 0)


def local_quads(n_seq, query_nope, query_rope, latents, key_up, value_up, query_offset, context_offset):
    tokens = query_nope.shape[0]
    kv = latents.shape[0]
    heads = key_up.shape[1] // HEAD_DIM
    pairs = n_seq // 2
    chunks = heads // 4 // CHUNK_HEADS
    width = CHUNK_HEADS * HEAD_DIM
    rope_width = CHUNK_HEADS * ROPE
    dma = pltpu.SemaphoreType.DMA
    bf16 = jnp.bfloat16
    return pl.pallas_call(
        functools.partial(kernel, pairs, chunks),
        out_shape=jax.ShapeDtypeStruct(query_nope.shape, bf16),
        in_specs=[pl.BlockSpec(memory_space=pltpu.SMEM)] * 2 + [pl.BlockSpec(memory_space=pltpu.HBM)] * 5,
        out_specs=pl.BlockSpec(memory_space=pl.ANY),
        scratch_shapes=[
            pltpu.VMEM((chunks, LATENT, 2 * width), bf16),
            pltpu.VMEM((4, chunks, tokens, width), bf16),
            pltpu.VMEM((4, chunks, tokens, rope_width), bf16),
            pltpu.VMEM((8, latents.shape[1], kv), bf16),
            pltpu.VMEM((4, 8, kv), jnp.int32),
            pltpu.VMEM((8 * kv, LATENT), bf16),
            pltpu.VMEM((2, 8 * kv, 2 * ROPE), bf16),
            pltpu.VMEM((CHUNK_HEADS, 8 * kv, 2 * HEAD_DIM), bf16),
            pltpu.VMEM((4, chunks, tokens, width), bf16),
            dma((2, chunks)), dma((chunks,)), dma((chunks,)), dma, dma((chunks,)),
            dma((2, chunks)), dma((2, chunks)), dma((4, chunks)), dma((4, chunks)), dma((4, chunks)), dma((4, chunks)),
            dma((4, 2)), dma((4, 2)), dma((4, 2)), dma((4, 2)), dma((4,)), dma((4,)),
            dma((chunks, pairs + 1)), dma((chunks, pairs + 1)), dma((chunks, pairs + 1)), dma((chunks, pairs + 1)),
            dma((4, chunks)), dma((4, chunks)),
        ],
        compiler_params=pltpu.CompilerParams(
            collective_id=0, has_side_effects=True, vmem_limit_bytes=62 * 1024 * 1024
        ),
        cost_estimate=pl.CostEstimate(flops=5 * 10 ** 9, bytes_accessed=8 * 10 ** 6, transcendentals=2 * 10 ** 6),
    )(query_offset, context_offset, query_nope, query_rope, latents.T, key_up, value_up)


def solution(mesh):
    in_specs = (
        P(("grp", "seq"), "head"),
        P(("grp", "seq"), "head"),
        P(("grp", "seq"), None),
        P("seq", "head"),
        P("seq", "head"),
        P(("grp", "seq")),
        P(("grp", "seq")),
    )
    out_specs = P(("grp", "seq"), "head")
    n_seq = mesh.shape["seq"]
    if mesh.shape["grp"] == 2 and n_seq % 2 == 0 and n_seq >= 6 and LATENT // n_seq % 16 == 0:
        local = functools.partial(local_quads, n_seq)
    else:
        local = local_general
    return jax.shard_map(local, mesh=mesh, in_specs=in_specs, out_specs=out_specs, check_vma=False)
```

```python
import functools
import math

import jax
import jax.numpy as jnp
from jax import lax
from jax.experimental import pallas as pl
from jax.experimental.pallas import tpu as pltpu
from jax.sharding import PartitionSpec as P

LATENT = 512
ROPE = 64
HEAD_DIM = 128
STEPS = 2
CHUNK_HEADS = 2
AHEAD = 2
MESH = pl.DeviceIdType.MESH


def shifted(x, axis, by):
    peers = lax.axis_size(axis)
    return lax.ppermute(x, axis, [(i, (i + by) % peers) for i in range(peers)])


def fetch_block(latent_block, distance):
    return shifted(latent_block, "seq", distance)


def local_general(query_nope, query_rope, latents, key_up, value_up, query_offset, context_offset):
    query_rows = query_nope.shape[0]
    kv_rows = latents.shape[0]
    local_heads = key_up.shape[1] // HEAD_DIM
    blocks = [latents]
    for distance in range(STEPS):
        blocks.append(fetch_block(blocks[-1], 1))
    context = jnp.concatenate(blocks, 0)
    latent_cols = context[:, :LATENT]
    rope_keys = context[:, LATENT:]
    key_full, value_full = (
        lax.all_gather(key_up, "seq", axis=0, tiled=True),
        lax.all_gather(value_up, "seq", axis=0, tiled=True),
    )
    key_sums = jnp.dot(latent_cols, key_full, preferred_element_type=jnp.float32)
    value_sums = jnp.dot(latent_cols, value_full, preferred_element_type=jnp.float32)
    key_rows = key_sums.astype(jnp.bfloat16).reshape(-1, local_heads, HEAD_DIM)
    value_rows = value_sums.astype(jnp.bfloat16).reshape(-1, local_heads, HEAD_DIM)
    query_part = query_nope.reshape(query_rows, local_heads, HEAD_DIM)
    rotary_part = query_rope.reshape(query_rows, local_heads, ROPE)
    softmax_scale = 1.0 / math.sqrt(HEAD_DIM + ROPE)
    scores = jnp.einsum("qhd,khd->hqk", query_part, key_rows, preferred_element_type=jnp.float32)
    scores = (
        scores
        + jnp.einsum("qhr,kr->hqk", rotary_part, rope_keys, preferred_element_type=jnp.float32)
    ) * softmax_scale
    query_place = query_offset[0] + jnp.arange(query_rows, dtype=jnp.int32)
    own_place = context_offset[0] + jnp.arange(kv_rows, dtype=jnp.int32)
    mask_list = [own_place[None, :] <= query_place[:, None]]
    for distance in range(STEPS):
        mask_list.append(jnp.ones((query_rows, kv_rows), dtype=bool))
    visible = jnp.concatenate(mask_list, 1)[None, :, :]
    scores = jnp.where(visible, scores, jnp.float32(-1e30))
    highest = jnp.max(scores, axis=2, keepdims=True)
    numerator = jnp.where(visible, jnp.exp(scores - highest), jnp.float32(0.0))
    denominator = jnp.sum(numerator, axis=2, keepdims=True)
    weights_bf = (numerator / denominator).astype(jnp.bfloat16)
    output = jnp.einsum("hqk,khd->qhd", weights_bf, value_rows, preferred_element_type=jnp.float32)
    return output.reshape(query_rows, local_heads * HEAD_DIM).astype(jnp.bfloat16)


def kernel(
    pairs, chunks, q_off, c_off, qn, qr, lat, ku, vu, out,
    w, q, r, blocks, offs, context, ropes, wide, o,
    own_w, own_q, own_r, own_lat_sem, own_o,
    xw_s, xw_r, q_s, q_r, r_s, r_r, lat_s, lat_r, twin_s, twin_r, off_s, off_r,
    right_s, right_r, left_s, left_r, o_s, o_r,
):
    g, s, c = lax.axis_index("grp"), lax.axis_index("seq"), lax.axis_index("head")
    z, x = s // 2, s % 2
    me = 2 * g + x
    mate = 2 * z + 1 - x
    shard = ku.shape[0]
    width = q.shape[3]
    rope_width = r.shape[3]
    lat_half = lat.shape[0] // 2
    to_mate = (g, mate, c)
    to_right = (g, 2 * ((z + 1) % pairs) + x, c)
    to_left = (g, 2 * ((z + pairs - 1) % pairs) + x, c)
    to_twin = (g, s, 1 - c)

    def member(k):
        kg, kx = k // 2, k % 2
        return g + kg - 2 * g * kg, x + kx - 2 * x * kx

    def to_member(k):
        mg, mx = member(k)
        return (mg, 2 * z + mx, c)

    def number(k):
        mg, mx = member(k)
        return 2 * mg + mx

    def remote(src, dst, send, recv, device):
        return pltpu.make_async_remote_copy(
            src_ref=src, dst_ref=dst, send_sem=send, recv_sem=recv, device_id=device, device_id_type=MESH
        )

    def cols(quarter, j):
        return pl.ds(pl.multiple_of((quarter * chunks + j) * width, 128), width)

    def rope_cols(quarter, j):
        return pl.ds(pl.multiple_of((quarter * chunks + j) * rope_width, 128), rope_width)

    def rows(first, count):
        return pl.ds(pl.multiple_of(first, 16), count)

    def own_copies(j):
        mine = rows(s * shard, shard)
        return [
            pltpu.make_async_copy(up.at[:, cols(me, j)], w.at[j, mine, m * width:(m + 1) * width], own_w.at[m, j])
            for m, up in enumerate((ku, vu))
        ]

    def mate_weights(j):
        mine = rows(s * shard, shard)
        quarter = 2 * g + 1 - x
        return [
            remote(
                up.at[:, cols(quarter, j)], w.at[j, mine, m * width:(m + 1) * width], xw_s.at[m, j], xw_r.at[m, j],
                to_mate,
            )
            for m, up in enumerate((ku, vu))
        ]

    def own_query(j):
        return [
            pltpu.make_async_copy(qn.at[:, cols(me, j)], q.at[me, j], own_q.at[j]),
            pltpu.make_async_copy(qr.at[:, rope_cols(me, j)], r.at[me, j], own_r.at[j]),
        ]

    def member_query(j):
        copies = []
        for k in range(1, 4):
            copies.append(remote(qn.at[:, cols(number(k), j)], q.at[me, j], q_s.at[k, j], q_r.at[k, j], to_member(k)))
            copies.append(remote(qr.at[:, rope_cols(number(k), j)], r.at[me, j], r_s.at[k, j], r_r.at[k, j], to_member(k)))
        return copies

    def payload(j, place):
        return w.at[j, rows(place * 2 * shard, 2 * shard), :]

    def go_right(j, d, source=None):
        if source is not None:
            ref = w.at[j, rows(source * shard, shard), :]
            slot = pairs * (source % 2)
            return remote(ref, ref, right_s.at[j, slot], right_r.at[j, slot], to_right)
        ref = payload(j, z - d + 1)
        return remote(ref, ref, right_s.at[j, d], right_r.at[j, d], to_right)

    def go_left(j, d, source=None):
        if source is not None:
            ref = w.at[j, rows(source * shard, shard), :]
            slot = pairs * (source % 2)
            return remote(ref, ref, left_s.at[j, slot], left_r.at[j, slot], to_left)
        ref = payload(j, z + d - 1)
        return remote(ref, ref, left_s.at[j, d], left_r.at[j, d], to_left)

    def place(k, current):
        mg, mx = member(k)
        return 4 * mg + 2 * current + mx

    def own_part(ref):
        return ref.at[rows(c * lat_half, lat_half), :]

    own_lat = pltpu.make_async_copy(lat, blocks.at[place(0, 1)], own_lat_sem)
    lat_right = remote(own_part(lat), own_part(blocks.at[place(0, 0)]), lat_s.at[0, 0], lat_r.at[0, 0], to_right)

    def lat_member(k, current):
        src = own_part(lat) if current else own_part(blocks.at[place(0, 0)])
        return remote(src, own_part(blocks.at[place(0, current)]), lat_s.at[k, current], lat_r.at[k, current], to_member(k))

    def lat_twin(k, current):
        ref = own_part(blocks.at[place(k, current)])
        return remote(ref, ref, twin_s.at[k, current], twin_r.at[k, current], to_twin)

    def off_member(k):
        return remote(offs.at[me], offs.at[me], off_s.at[k], off_r.at[k], to_member(k))

    def result_own(j):
        return pltpu.make_async_copy(o.at[me, j], out.at[:, cols(me, j)], own_o.at[j])

    def result_member(j, k):
        return remote(o.at[number(k), j], out.at[:, cols(me, j)], o_s.at[k, j], o_r.at[k, j], to_member(k))

    def start_own(j, carry):
        for copy in own_copies(j):
            copy.start()
        return carry

    lax.fori_loop(0, chunks, start_own, 0)
    own_lat.start()
    offs[me] = jnp.full(offs.shape[1:], q_off[0] - c_off[0], jnp.int32)

    barrier = pltpu.get_barrier_semaphore()
    for device in [to_member(k) for k in range(1, 4)] + [to_right, to_left, to_twin]:
        pl.semaphore_signal(barrier, inc=1, device_id=device, device_id_type=MESH)
    pl.semaphore_wait(barrier, 6)

    def start_mate(j, carry):
        for copy in mate_weights(j):
            copy.start()
        return carry

    def send(j, source):
        @pl.when(z + 1 < pairs)
        def _():
            go_right(j, 1, source).start()

        @pl.when(z > 0)
        def _():
            go_left(j, 1, source).start()

    def enter(j):
        for copy in own_copies(j):
            copy.wait()
        send(j, s)

    def pass_mate(j):
        for copy in mate_weights(j):
            copy.wait_recv()
        send(j, mate)

    def ask(j, carry):
        for copy in own_query(j) + member_query(j):
            copy.start()
        return carry

    def first(j, carry):
        enter(j)
        return carry

    def second(j, carry):
        pass_mate(j)
        return carry

    lat_right.start()
    for k in range(3, 0, -1):
        lat_member(k, 1).start()
        off_member(k).start()
    lax.fori_loop(0, chunks, start_mate, 0)
    lax.fori_loop(0, AHEAD, first, 0)
    def spread_previous():
        lat_right.wait_recv()
        for k in range(1, 4):
            lat_member(k, 0).start()
        lat_twin(0, 0).start()

    lax.fori_loop(0, AHEAD, second, 0)
    spread_previous()
    lax.fori_loop(0, 1, ask, 0)

    def hand_on(j, d):
        @pl.when(z >= d)
        def _():
            if d == 1:
                go_right(j, d, s).wait_recv()
                go_right(j, d, mate).wait_recv()
            else:
                go_right(j, d).wait_recv()

            @pl.when(z + 1 < pairs)
            def _():
                if d + 1 < pairs:
                    go_right(j, d + 1).start()

        @pl.when(z + d < pairs)
        def _():
            if d == 1:
                go_left(j, d, s).wait_recv()
                go_left(j, d, mate).wait_recv()
            else:
                go_left(j, d).wait_recv()

            @pl.when(z > 0)
            def _():
                if d + 1 < pairs:
                    go_left(j, d + 1).start()

    def spread_twin():
        for k in range(1, 4):
            for current in (1, 0):
                lat_member(k, current).wait_recv()
                lat_twin(k, current).start()

    def prepare():
        own_lat.wait()
        lat_twin(0, 0).wait_recv()
        for k in range(1, 4):
            off_member(k).wait_recv()
            for current in (1, 0):
                lat_twin(k, current).wait_recv()
        kv = lat.shape[1]
        none = jnp.zeros((kv, ROPE), jnp.bfloat16)
        for k in range(8):
            context[k * kv:(k + 1) * kv, :] = blocks[k, :LATENT, :].T
            rope_keys = blocks[k, LATENT:, :].T
            ropes[0, k * kv:(k + 1) * kv, :] = jnp.concatenate([rope_keys, none], 1)
            ropes[1, k * kv:(k + 1) * kv, :] = jnp.concatenate([none, rope_keys], 1)
        wide[:, :, HEAD_DIM:] = jnp.ones((wide.shape[0], 8 * kv, HEAD_DIM), jnp.bfloat16)

    def attend(j):
        for copy in own_query(j):
            copy.wait()
        for copy in member_query(j):
            copy.wait_recv()
        kv = lat.shape[1]
        tokens = qn.shape[0]
        both = jnp.dot(context[...], w[j], preferred_element_type=jnp.float32).astype(jnp.bfloat16)
        for h in range(width // HEAD_DIM):
            wide[h, :, :HEAD_DIM] = both[:, width + h * HEAD_DIM:width + (h + 1) * HEAD_DIM]
        factor = math.log2(math.e) / math.sqrt(HEAD_DIM + ROPE)
        token = lax.broadcasted_iota(jnp.int32, (tokens, kv), 0)
        row = lax.broadcasted_iota(jnp.int32, (tokens, kv), 1)
        pieces = [(b, h) for b in range(4) for h in range(width // HEAD_DIM)]

        def seen(b):
            start = (4 * (b // 2) + b % 2) * kv
            return slice(start, start + (1 + STEPS) * kv)

        def lanes(h):
            return slice(h * HEAD_DIM, (h + 1) * HEAD_DIM)

        scored = []
        for b, h in pieces:
            pair_lanes = slice(h // 2 * 2 * ROPE, (h // 2 + 1) * 2 * ROPE)
            query = jnp.concatenate([q[b, j, :, lanes(h)], r[b, j, :, pair_lanes]], 1)
            key = jnp.concatenate([both[seen(b), lanes(h)], ropes[h % 2, seen(b), :]], 1)
            scored.append(
                lax.dot_general(query, key, (((1,), (1,)), ((), ())), preferred_element_type=jnp.float32)
            )
        numerators = []
        for (b, h), scores in zip(pieces, scored):
            visible = row <= token + offs[b, 0:1, :]
            scores = jnp.concatenate(
                [scores[:, :STEPS * kv], jnp.where(visible, scores[:, STEPS * kv:], jnp.float32(-1e30))], 1
            )
            highest = jnp.max(scores, axis=1, keepdims=True)
            numerators.append(jnp.exp2((scores - highest) * factor).astype(jnp.bfloat16))
        sums = [
            jnp.dot(numerator, wide[h, seen(b), :], preferred_element_type=jnp.float32)
            for (b, h), numerator in zip(pieces, numerators)
        ]
        for (b, h), summed in zip(pieces, sums):
            o[b, j, :, lanes(h)] = (summed[:, :HEAD_DIM] / summed[:, HEAD_DIM:]).astype(jnp.bfloat16)
        for k in range(3, 0, -1):
            result_member(j, k).start()
        result_own(j).start()

    def step(t, carry):
        @pl.when(t + AHEAD < chunks)
        def _():
            enter(t + AHEAD)
            pass_mate(t + AHEAD)

        @pl.when(t + 1 < chunks)
        def _():
            ask(t + 1, 0)

        for d in range(1, pairs):
            @pl.when((t >= d) & (t < chunks + d))
            def _():
                hand_on(t - d, d)

        @pl.when(t == 1)
        def _():
            spread_twin()

        @pl.when(t == pairs - 1)
        def _():
            prepare()

        @pl.when(t >= pairs - 1)
        def _():
            attend(t - pairs + 1)

        return carry

    lax.fori_loop(0, chunks + pairs - 1, step, 0)

    lat_right.wait_send()
    lat_twin(0, 0).wait_send()
    for k in range(1, 4):
        off_member(k).wait_send()
        for current in (1, 0):
            lat_member(k, current).wait_send()
            lat_twin(k, current).wait_send()

    def finish(j, carry):
        for copy in mate_weights(j) + member_query(j):
            copy.wait_send()
        for d in range(1, pairs):
            @pl.when((z >= d - 1) & (z + 1 < pairs))
            def _():
                if d == 1:
                    go_right(j, d, s).wait_send()
                    go_right(j, d, mate).wait_send()
                else:
                    go_right(j, d).wait_send()

            @pl.when((z + d - 1 < pairs) & (z > 0))
            def _():
                if d == 1:
                    go_left(j, d, s).wait_send()
                    go_left(j, d, mate).wait_send()
                else:
                    go_left(j, d).wait_send()

        result_own(j).wait()
        for k in range(1, 4):
            result_member(j, k).wait()
        return carry

    lax.fori_loop(0, chunks, finish, 0)


def local_quads(n_seq, query_nope, query_rope, latents, key_up, value_up, query_offset, context_offset):
    tokens = query_nope.shape[0]
    kv = latents.shape[0]
    heads = key_up.shape[1] // HEAD_DIM
    pairs = n_seq // 2
    chunks = heads // 4 // CHUNK_HEADS
    width = CHUNK_HEADS * HEAD_DIM
    rope_width = CHUNK_HEADS * ROPE
    dma = pltpu.SemaphoreType.DMA
    bf16 = jnp.bfloat16
    return pl.pallas_call(
        functools.partial(kernel, pairs, chunks),
        out_shape=jax.ShapeDtypeStruct(query_nope.shape, bf16),
        in_specs=[pl.BlockSpec(memory_space=pltpu.SMEM)] * 2 + [pl.BlockSpec(memory_space=pltpu.HBM)] * 5,
        out_specs=pl.BlockSpec(memory_space=pl.ANY),
        scratch_shapes=[
            pltpu.VMEM((chunks, LATENT, 2 * width), bf16),
            pltpu.VMEM((4, chunks, tokens, width), bf16),
            pltpu.VMEM((4, chunks, tokens, rope_width), bf16),
            pltpu.VMEM((8, latents.shape[1], kv), bf16),
            pltpu.VMEM((4, 8, kv), jnp.int32),
            pltpu.VMEM((8 * kv, LATENT), bf16),
            pltpu.VMEM((2, 8 * kv, 2 * ROPE), bf16),
            pltpu.VMEM((CHUNK_HEADS, 8 * kv, 2 * HEAD_DIM), bf16),
            pltpu.VMEM((4, chunks, tokens, width), bf16),
            dma((2, chunks)), dma((chunks,)), dma((chunks,)), dma, dma((chunks,)),
            dma((2, chunks)), dma((2, chunks)), dma((4, chunks)), dma((4, chunks)), dma((4, chunks)), dma((4, chunks)),
            dma((4, 2)), dma((4, 2)), dma((4, 2)), dma((4, 2)), dma((4,)), dma((4,)),
            dma((chunks, pairs + 1)), dma((chunks, pairs + 1)), dma((chunks, pairs + 1)), dma((chunks, pairs + 1)),
            dma((4, chunks)), dma((4, chunks)),
        ],
        compiler_params=pltpu.CompilerParams(
            collective_id=0, has_side_effects=True, vmem_limit_bytes=62 * 1024 * 1024
        ),
        cost_estimate=pl.CostEstimate(flops=5 * 10 ** 9, bytes_accessed=8 * 10 ** 6, transcendentals=2 * 10 ** 6),
    )(query_offset, context_offset, query_nope, query_rope, latents.T, key_up, value_up)


def solution(mesh):
    in_specs = (
        P(("grp", "seq"), "head"),
        P(("grp", "seq"), "head"),
        P(("grp", "seq"), None),
        P("seq", "head"),
        P("seq", "head"),
        P(("grp", "seq")),
        P(("grp", "seq")),
    )
    out_specs = P(("grp", "seq"), "head")
    n_seq = mesh.shape["seq"]
    if mesh.shape["grp"] == 2 and n_seq % 2 == 0 and n_seq >= 6 and LATENT // n_seq % 16 == 0:
        local = functools.partial(local_quads, n_seq)
    else:
        local = local_general
    return jax.shard_map(local, mesh=mesh, in_specs=in_specs, out_specs=out_specs, check_vma=False)
```

```python
import functools
import math

import jax
import jax.numpy as jnp
from jax import lax
from jax.experimental import pallas as pl
from jax.experimental.pallas import tpu as pltpu
from jax.sharding import PartitionSpec as P

LATENT = 512
ROPE = 64
HEAD_DIM = 128
STEPS = 2
CHUNK_HEADS = 2
AHEAD = 2
MESH = pl.DeviceIdType.MESH


def shifted(x, axis, by):
    peers = lax.axis_size(axis)
    return lax.ppermute(x, axis, [(i, (i + by) % peers) for i in range(peers)])


def fetch_block(latent_block, distance):
    return shifted(latent_block, "seq", distance)


def local_general(query_nope, query_rope, latents, key_up, value_up, query_offset, context_offset):
    query_rows = query_nope.shape[0]
    kv_rows = latents.shape[0]
    local_heads = key_up.shape[1] // HEAD_DIM
    blocks = [latents]
    for distance in range(STEPS):
        blocks.append(fetch_block(blocks[-1], 1))
    context = jnp.concatenate(blocks, 0)
    latent_cols = context[:, :LATENT]
    rope_keys = context[:, LATENT:]
    key_full, value_full = (
        lax.all_gather(key_up, "seq", axis=0, tiled=True),
        lax.all_gather(value_up, "seq", axis=0, tiled=True),
    )
    key_sums = jnp.dot(latent_cols, key_full, preferred_element_type=jnp.float32)
    value_sums = jnp.dot(latent_cols, value_full, preferred_element_type=jnp.float32)
    key_rows = key_sums.astype(jnp.bfloat16).reshape(-1, local_heads, HEAD_DIM)
    value_rows = value_sums.astype(jnp.bfloat16).reshape(-1, local_heads, HEAD_DIM)
    query_part = query_nope.reshape(query_rows, local_heads, HEAD_DIM)
    rotary_part = query_rope.reshape(query_rows, local_heads, ROPE)
    softmax_scale = 1.0 / math.sqrt(HEAD_DIM + ROPE)
    scores = jnp.einsum("qhd,khd->hqk", query_part, key_rows, preferred_element_type=jnp.float32)
    scores = (
        scores
        + jnp.einsum("qhr,kr->hqk", rotary_part, rope_keys, preferred_element_type=jnp.float32)
    ) * softmax_scale
    query_place = query_offset[0] + jnp.arange(query_rows, dtype=jnp.int32)
    own_place = context_offset[0] + jnp.arange(kv_rows, dtype=jnp.int32)
    mask_list = [own_place[None, :] <= query_place[:, None]]
    for distance in range(STEPS):
        mask_list.append(jnp.ones((query_rows, kv_rows), dtype=bool))
    visible = jnp.concatenate(mask_list, 1)[None, :, :]
    scores = jnp.where(visible, scores, jnp.float32(-1e30))
    highest = jnp.max(scores, axis=2, keepdims=True)
    numerator = jnp.where(visible, jnp.exp(scores - highest), jnp.float32(0.0))
    denominator = jnp.sum(numerator, axis=2, keepdims=True)
    weights_bf = (numerator / denominator).astype(jnp.bfloat16)
    output = jnp.einsum("hqk,khd->qhd", weights_bf, value_rows, preferred_element_type=jnp.float32)
    return output.reshape(query_rows, local_heads * HEAD_DIM).astype(jnp.bfloat16)


def kernel(
    pairs, chunks, q_off, c_off, qn, qr, lat, ku, vu, out,
    w, q, r, blocks, offs, context, ropes, wide, o,
    own_w, own_q, own_r, own_lat_sem, own_o,
    xw_s, xw_r, q_s, q_r, r_s, r_r, lat_s, lat_r, twin_s, twin_r, off_s, off_r,
    right_s, right_r, left_s, left_r, o_s, o_r,
):
    g, s, c = lax.axis_index("grp"), lax.axis_index("seq"), lax.axis_index("head")
    z, x = s // 2, s % 2
    me = 2 * g + x
    mate = 2 * z + 1 - x
    shard = ku.shape[0]
    width = q.shape[3]
    rope_width = r.shape[3]
    lat_half = lat.shape[0] // 2
    to_mate = (g, mate, c)
    to_right = (g, 2 * ((z + 1) % pairs) + x, c)
    to_left = (g, 2 * ((z + pairs - 1) % pairs) + x, c)
    to_twin = (g, s, 1 - c)

    def member(k):
        kg, kx = k // 2, k % 2
        return g + kg - 2 * g * kg, x + kx - 2 * x * kx

    def to_member(k):
        mg, mx = member(k)
        return (mg, 2 * z + mx, c)

    def number(k):
        mg, mx = member(k)
        return 2 * mg + mx

    def remote(src, dst, send, recv, device):
        return pltpu.make_async_remote_copy(
            src_ref=src, dst_ref=dst, send_sem=send, recv_sem=recv, device_id=device, device_id_type=MESH
        )

    def cols(quarter, j):
        return pl.ds(pl.multiple_of((quarter * chunks + j) * width, 128), width)

    def rope_cols(quarter, j):
        return pl.ds(pl.multiple_of((quarter * chunks + j) * rope_width, 128), rope_width)

    def rows(first, count):
        return pl.ds(pl.multiple_of(first, 16), count)

    def own_copies(j):
        mine = rows(s * shard, shard)
        return [
            pltpu.make_async_copy(up.at[:, cols(me, j)], w.at[j, mine, m * width:(m + 1) * width], own_w.at[m, j])
            for m, up in enumerate((ku, vu))
        ]

    def mate_weights(j):
        mine = rows(s * shard, shard)
        quarter = 2 * g + 1 - x
        return [
            remote(
                up.at[:, cols(quarter, j)], w.at[j, mine, m * width:(m + 1) * width], xw_s.at[m, j], xw_r.at[m, j],
                to_mate,
            )
            for m, up in enumerate((ku, vu))
        ]

    def own_query(j):
        return [
            pltpu.make_async_copy(qn.at[:, cols(me, j)], q.at[me, j], own_q.at[j]),
            pltpu.make_async_copy(qr.at[:, rope_cols(me, j)], r.at[me, j], own_r.at[j]),
        ]

    def member_query(j):
        copies = []
        for k in range(1, 4):
            copies.append(remote(qn.at[:, cols(number(k), j)], q.at[me, j], q_s.at[k, j], q_r.at[k, j], to_member(k)))
            copies.append(remote(qr.at[:, rope_cols(number(k), j)], r.at[me, j], r_s.at[k, j], r_r.at[k, j], to_member(k)))
        return copies

    def payload(j, place):
        return w.at[j, rows(place * 2 * shard, 2 * shard), :]

    def go_right(j, d, source=None):
        if source is not None:
            ref = w.at[j, rows(source * shard, shard), :]
            slot = pairs * (source % 2)
            return remote(ref, ref, right_s.at[j, slot], right_r.at[j, slot], to_right)
        ref = payload(j, z - d + 1)
        return remote(ref, ref, right_s.at[j, d], right_r.at[j, d], to_right)

    def go_left(j, d, source=None):
        if source is not None:
            ref = w.at[j, rows(source * shard, shard), :]
            slot = pairs * (source % 2)
            return remote(ref, ref, left_s.at[j, slot], left_r.at[j, slot], to_left)
        ref = payload(j, z + d - 1)
        return remote(ref, ref, left_s.at[j, d], left_r.at[j, d], to_left)

    def place(k, current):
        mg, mx = member(k)
        return 4 * mg + 2 * current + mx

    def own_part(ref):
        return ref.at[rows(c * lat_half, lat_half), :]

    own_lat = pltpu.make_async_copy(lat, blocks.at[place(0, 1)], own_lat_sem)
    lat_right = remote(own_part(lat), own_part(blocks.at[place(0, 0)]), lat_s.at[0, 0], lat_r.at[0, 0], to_right)

    def lat_member(k, current):
        src = own_part(lat) if current else own_part(blocks.at[place(0, 0)])
        return remote(src, own_part(blocks.at[place(0, current)]), lat_s.at[k, current], lat_r.at[k, current], to_member(k))

    def lat_twin(k, current):
        ref = own_part(blocks.at[place(k, current)])
        return remote(ref, ref, twin_s.at[k, current], twin_r.at[k, current], to_twin)

    def off_member(k):
        return remote(offs.at[me], offs.at[me], off_s.at[k], off_r.at[k], to_member(k))

    def result_own(j):
        return pltpu.make_async_copy(o.at[me, j], out.at[:, cols(me, j)], own_o.at[j])

    def result_member(j, k):
        return remote(o.at[number(k), j], out.at[:, cols(me, j)], o_s.at[k, j], o_r.at[k, j], to_member(k))

    def start_own(j, carry):
        for copy in own_copies(j):
            copy.start()
        return carry

    lax.fori_loop(0, chunks, start_own, 0)
    own_lat.start()
    offs[me] = jnp.full(offs.shape[1:], q_off[0] - c_off[0], jnp.int32)

    barrier = pltpu.get_barrier_semaphore()
    for device in [to_member(k) for k in range(1, 4)] + [to_right, to_left, to_twin]:
        pl.semaphore_signal(barrier, inc=1, device_id=device, device_id_type=MESH)
    pl.semaphore_wait(barrier, 6)

    def start_mate(j, carry):
        for copy in mate_weights(j):
            copy.start()
        return carry

    def send(j, source):
        @pl.when(z + 1 < pairs)
        def _():
            go_right(j, 1, source).start()

        @pl.when(z > 0)
        def _():
            go_left(j, 1, source).start()

    def enter(j):
        for copy in own_copies(j):
            copy.wait()
        send(j, s)

    def pass_mate(j):
        for copy in mate_weights(j):
            copy.wait_recv()
        send(j, mate)

    def ask(j, carry):
        for copy in own_query(j) + member_query(j):
            copy.start()
        return carry

    def first(j, carry):
        enter(j)
        return carry

    def second(j, carry):
        pass_mate(j)
        return carry

    lat_right.start()
    lax.fori_loop(0, AHEAD, first, 0)
    lax.fori_loop(0, chunks, start_mate, 0)
    for k in range(3, 0, -1):
        lat_member(k, 1).start()
        off_member(k).start()
    def spread_previous():
        lat_right.wait_recv()
        for k in range(1, 4):
            lat_member(k, 0).start()
        lat_twin(0, 0).start()

    lax.fori_loop(0, AHEAD, second, 0)
    spread_previous()
    lax.fori_loop(0, 1, ask, 0)

    def hand_on(j, d):
        @pl.when(z >= d)
        def _():
            if d == 1:
                go_right(j, d, s).wait_recv()
                go_right(j, d, mate).wait_recv()
            else:
                go_right(j, d).wait_recv()

            @pl.when(z + 1 < pairs)
            def _():
                if d + 1 < pairs:
                    go_right(j, d + 1).start()

        @pl.when(z + d < pairs)
        def _():
            if d == 1:
                go_left(j, d, s).wait_recv()
                go_left(j, d, mate).wait_recv()
            else:
                go_left(j, d).wait_recv()

            @pl.when(z > 0)
            def _():
                if d + 1 < pairs:
                    go_left(j, d + 1).start()

    def spread_twin():
        for k in range(1, 4):
            for current in (1, 0):
                lat_member(k, current).wait_recv()
                lat_twin(k, current).start()

    def prepare():
        own_lat.wait()
        lat_twin(0, 0).wait_recv()
        for k in range(1, 4):
            off_member(k).wait_recv()
            for current in (1, 0):
                lat_twin(k, current).wait_recv()
        kv = lat.shape[1]
        none = jnp.zeros((kv, ROPE), jnp.bfloat16)
        for k in range(8):
            context[k * kv:(k + 1) * kv, :] = blocks[k, :LATENT, :].T
            rope_keys = blocks[k, LATENT:, :].T
            ropes[0, k * kv:(k + 1) * kv, :] = jnp.concatenate([rope_keys, none], 1)
            ropes[1, k * kv:(k + 1) * kv, :] = jnp.concatenate([none, rope_keys], 1)
        wide[:, :, HEAD_DIM:] = jnp.ones((wide.shape[0], 8 * kv, HEAD_DIM), jnp.bfloat16)

    def attend(j):
        for copy in own_query(j):
            copy.wait()
        for copy in member_query(j):
            copy.wait_recv()
        kv = lat.shape[1]
        tokens = qn.shape[0]
        both = jnp.dot(context[...], w[j], preferred_element_type=jnp.float32).astype(jnp.bfloat16)
        for h in range(width // HEAD_DIM):
            wide[h, :, :HEAD_DIM] = both[:, width + h * HEAD_DIM:width + (h + 1) * HEAD_DIM]
        factor = math.log2(math.e) / math.sqrt(HEAD_DIM + ROPE)
        token = lax.broadcasted_iota(jnp.int32, (tokens, kv), 0)
        row = lax.broadcasted_iota(jnp.int32, (tokens, kv), 1)
        pieces = [(b, h) for b in range(4) for h in range(width // HEAD_DIM)]

        def seen(b):
            start = (4 * (b // 2) + b % 2) * kv
            return slice(start, start + (1 + STEPS) * kv)

        def lanes(h):
            return slice(h * HEAD_DIM, (h + 1) * HEAD_DIM)

        scored = []
        for b, h in pieces:
            pair_lanes = slice(h // 2 * 2 * ROPE, (h // 2 + 1) * 2 * ROPE)
            query = jnp.concatenate([q[b, j, :, lanes(h)], r[b, j, :, pair_lanes]], 1)
            key = jnp.concatenate([both[seen(b), lanes(h)], ropes[h % 2, seen(b), :]], 1)
            scored.append(
                lax.dot_general(query, key, (((1,), (1,)), ((), ())), preferred_element_type=jnp.float32)
            )
        numerators = []
        for (b, h), scores in zip(pieces, scored):
            visible = row <= token + offs[b, 0:1, :]
            scores = jnp.concatenate(
                [scores[:, :STEPS * kv], jnp.where(visible, scores[:, STEPS * kv:], jnp.float32(-1e30))], 1
            )
            highest = jnp.max(scores, axis=1, keepdims=True)
            numerators.append(jnp.exp2((scores - highest) * factor).astype(jnp.bfloat16))
        sums = [
            jnp.dot(numerator, wide[h, seen(b), :], preferred_element_type=jnp.float32)
            for (b, h), numerator in zip(pieces, numerators)
        ]
        for (b, h), summed in zip(pieces, sums):
            o[b, j, :, lanes(h)] = (summed[:, :HEAD_DIM] / summed[:, HEAD_DIM:]).astype(jnp.bfloat16)
        for k in range(3, 0, -1):
            result_member(j, k).start()
        result_own(j).start()

    def step(t, carry):
        @pl.when(t + AHEAD < chunks)
        def _():
            enter(t + AHEAD)
            pass_mate(t + AHEAD)

        @pl.when(t + 1 < chunks)
        def _():
            ask(t + 1, 0)

        for d in range(1, pairs):
            @pl.when((t >= d) & (t < chunks + d))
            def _():
                hand_on(t - d, d)

        @pl.when(t == 1)
        def _():
            spread_twin()

        @pl.when(t == pairs - 1)
        def _():
            prepare()

        @pl.when(t >= pairs - 1)
        def _():
            attend(t - pairs + 1)

        return carry

    lax.fori_loop(0, chunks + pairs - 1, step, 0)

    lat_right.wait_send()
    lat_twin(0, 0).wait_send()
    for k in range(1, 4):
        off_member(k).wait_send()
        for current in (1, 0):
            lat_member(k, current).wait_send()
            lat_twin(k, current).wait_send()

    def finish(j, carry):
        for copy in mate_weights(j) + member_query(j):
            copy.wait_send()
        for d in range(1, pairs):
            @pl.when((z >= d - 1) & (z + 1 < pairs))
            def _():
                if d == 1:
                    go_right(j, d, s).wait_send()
                    go_right(j, d, mate).wait_send()
                else:
                    go_right(j, d).wait_send()

            @pl.when((z + d - 1 < pairs) & (z > 0))
            def _():
                if d == 1:
                    go_left(j, d, s).wait_send()
                    go_left(j, d, mate).wait_send()
                else:
                    go_left(j, d).wait_send()

        result_own(j).wait()
        for k in range(1, 4):
            result_member(j, k).wait()
        return carry

    lax.fori_loop(0, chunks, finish, 0)


def local_quads(n_seq, query_nope, query_rope, latents, key_up, value_up, query_offset, context_offset):
    tokens = query_nope.shape[0]
    kv = latents.shape[0]
    heads = key_up.shape[1] // HEAD_DIM
    pairs = n_seq // 2
    chunks = heads // 4 // CHUNK_HEADS
    width = CHUNK_HEADS * HEAD_DIM
    rope_width = CHUNK_HEADS * ROPE
    dma = pltpu.SemaphoreType.DMA
    bf16 = jnp.bfloat16
    return pl.pallas_call(
        functools.partial(kernel, pairs, chunks),
        out_shape=jax.ShapeDtypeStruct(query_nope.shape, bf16),
        in_specs=[pl.BlockSpec(memory_space=pltpu.SMEM)] * 2 + [pl.BlockSpec(memory_space=pltpu.HBM)] * 5,
        out_specs=pl.BlockSpec(memory_space=pl.ANY),
        scratch_shapes=[
            pltpu.VMEM((chunks, LATENT, 2 * width), bf16),
            pltpu.VMEM((4, chunks, tokens, width), bf16),
            pltpu.VMEM((4, chunks, tokens, rope_width), bf16),
            pltpu.VMEM((8, latents.shape[1], kv), bf16),
            pltpu.VMEM((4, 8, kv), jnp.int32),
            pltpu.VMEM((8 * kv, LATENT), bf16),
            pltpu.VMEM((2, 8 * kv, 2 * ROPE), bf16),
            pltpu.VMEM((CHUNK_HEADS, 8 * kv, 2 * HEAD_DIM), bf16),
            pltpu.VMEM((4, chunks, tokens, width), bf16),
            dma((2, chunks)), dma((chunks,)), dma((chunks,)), dma, dma((chunks,)),
            dma((2, chunks)), dma((2, chunks)), dma((4, chunks)), dma((4, chunks)), dma((4, chunks)), dma((4, chunks)),
            dma((4, 2)), dma((4, 2)), dma((4, 2)), dma((4, 2)), dma((4,)), dma((4,)),
            dma((chunks, pairs + 1)), dma((chunks, pairs + 1)), dma((chunks, pairs + 1)), dma((chunks, pairs + 1)),
            dma((4, chunks)), dma((4, chunks)),
        ],
        compiler_params=pltpu.CompilerParams(
            collective_id=0, has_side_effects=True, vmem_limit_bytes=62 * 1024 * 1024
        ),
        cost_estimate=pl.CostEstimate(flops=5 * 10 ** 9, bytes_accessed=8 * 10 ** 6, transcendentals=2 * 10 ** 6),
    )(query_offset, context_offset, query_nope, query_rope, latents.T, key_up, value_up)


def solution(mesh):
    in_specs = (
        P(("grp", "seq"), "head"),
        P(("grp", "seq"), "head"),
        P(("grp", "seq"), None),
        P("seq", "head"),
        P("seq", "head"),
        P(("grp", "seq")),
        P(("grp", "seq")),
    )
    out_specs = P(("grp", "seq"), "head")
    n_seq = mesh.shape["seq"]
    if mesh.shape["grp"] == 2 and n_seq % 2 == 0 and n_seq >= 6 and LATENT // n_seq % 16 == 0:
        local = functools.partial(local_quads, n_seq)
    else:
        local = local_general
    return jax.shard_map(local, mesh=mesh, in_specs=in_specs, out_specs=out_specs, check_vma=False)
```
